32 devices in a mesh: dp: 16 (over z, x, core), tensor: 2 (over y).
Axes of the slice: x: 2, y: 2, z: 4, core: 2. Of those that a mesh axis runs over, the one named last changes fastest.
Arguments:
- hidden_in: bfloat16 [4096, 4096], P(('dp', 'tensor')), may hold values from -12 to 12
- norm_gain: bfloat16 [4096], replicated, may hold values from 0.5 to 1.5
- w_query: bfloat16 [4096, 4096], P('dp', 'tensor'), may hold values from -0.11328125 to 0.11328125
- w_key: bfloat16 [4096, 1024], P('dp', 'tensor'), may hold values from -0.11328125 to 0.11328125
- w_value: bfloat16 [4096, 1024], P('dp', 'tensor'), may hold values from -0.09375 to 0.09375
- w_out: bfloat16 [4096, 4096], P('tensor', 'dp'), may hold values from -0.09375 to 0.09375
- segment: int32 [4096], P('dp'), may hold values from -1 to 1, as said below
Outputs:
- hidden_out: bfloat16 [4096, 4096], P(('dp', 'tensor'))
- kv_cache: bfloat16 [4096, 8, 256], P('dp', 'tensor')
The draws below stay inside these ranges and needn't reach their ends.
Inputs may be any that keep to these rules, and one draw needn't show every extreme that they name: `segment`: within each pack of 256 rows, prompts are numbered from 0 in order and each starts at a multiple of 128; a prompt's last tile may end in rows of -1, and whole tiles of -1 may only follow the last prompt of a pack; the first tile of every pack holds a prompt; in every draw some pack has no tile of -1 only and holds one prompt a tile.
All inputs are finite; a program needn't handle non-finite values.
Results may differ from the reference program's by a relative error of at most 0.0085.
Values may be sent and summed in bfloat16 or wider, within the bound.
A program may use at most 128 MiB of HBM per device.

```python
import jax
import jax.numpy as jnp
from jax import lax

D = 4096
HQ = 32
KVH = 8
HEAD = 128
TILE = 128
PACK = 256
TOKENS = 4096
N_DP = 16
N_TENSOR = 2


def draw_hidden_in(key, part):
    own_key = jax.random.fold_in(key, 1)
    values = jnp.clip(jax.random.normal(own_key, (TOKENS, D), jnp.float32), -6.0, 6.0)
    return values.astype(jnp.bfloat16)


def draw_w_query(key, part):
    values = jnp.clip(jax.random.normal(jax.random.fold_in(key, 2), (D, HQ * HEAD), jnp.float32), -6.0, 6.0) * D ** (-0.5)
    return values.astype(jnp.bfloat16)


def draw_w_key(key, part):
    values = jnp.clip(jax.random.normal(jax.random.fold_in(key, 3), (D, KVH * HEAD), jnp.float32), -6.0, 6.0) * D ** (-0.5)
    return values.astype(jnp.bfloat16)


def draw_segment(key, part):
    shards = TOKENS // PACK
    tile_count = PACK // TILE
    key_full, key_live, key_start, key_pad = jax.random.split(jax.random.fold_in(key, 4), 4)
    fullest = jax.random.randint(key_full, (), 0, shards)
    is_fullest = jnp.arange(shards) == fullest
    live_tiles = jax.random.randint(key_live, (shards,), 1, tile_count + 1)
    live_tiles = jnp.where(is_fullest, tile_count, live_tiles)
    starts = jax.random.randint(key_start, (shards, tile_count), 0, 2)
    starts = jnp.where(is_fullest[:, None], 1, starts)
    starts = starts.at[:, 0].set(1)
    tile_index = jnp.arange(tile_count)[None, :]
    tile_alive = tile_index < live_tiles[:, None]
    tile_segment = jnp.cumsum(starts, axis=1) - 1
    next_start = jnp.concatenate([starts[:, 1:], jnp.ones((shards, 1), jnp.int32)], axis=1)
    last_tile = (next_start == 1) | (tile_index == live_tiles[:, None] - 1)
    pad_length = jax.random.randint(key_pad, (shards, tile_count), 0, TILE)
    offset = jnp.arange(TILE)[None, None, :]
    is_padding = last_tile[:, :, None] & (offset >= TILE - pad_length[:, :, None])
    segment_ids = jnp.where(tile_alive[:, :, None] & jnp.logical_not(is_padding), tile_segment[:, :, None], -1)
    return segment_ids.reshape(TOKENS).astype(jnp.int32)


def level_of(key, dims, cuts, low, top_value):
    def one(axis_at, blocks):
        heights = jax.random.uniform(jax.random.fold_in(jax.random.fold_in(key, 6), axis_at), (blocks,), jnp.float32, low / len(cuts), top_value / len(cuts))
        return jnp.repeat(jnp.exp(heights), dims[axis_at] // blocks).reshape((-1,) + (1,) * (len(dims) - axis_at - 1))

    gain = one(*cuts[0])
    for cut in cuts[1:]:
        gain = gain * one(*cut)
    return gain


def noise(key, dims, width, limit, cuts=(), kind=jnp.bfloat16):
    drawn = width * jax.random.normal(key, dims, jnp.float32)
    if cuts:
        drawn = drawn * level_of(key, dims, cuts, -0.22, 0.18)
    return jnp.clip(drawn, -limit, limit).astype(kind)


def setup_inputs(seed: int = 0) -> dict:
    key_of = jax.random.split(jax.random.key(seed), 8)
    hidden_in = draw_hidden_in(jax.random.fold_in(key_of[7], 71), 0)
    norm_gain = jnp.clip(1.0 + 0.1 * jax.random.normal(key_of[1], (D,), jnp.float32), 0.5, 1.5).astype(jnp.bfloat16)
    w_query = draw_w_query(jax.random.fold_in(key_of[7], 71), 0)
    w_key = draw_w_key(jax.random.fold_in(key_of[7], 71), 0)
    w_value = noise(key_of[4], (D, KVH * HEAD), D ** -0.5, 0.09375, ((0, 16), (1, 2)))
    w_out = noise(key_of[5], (HQ * HEAD, D), (HQ * HEAD) ** -0.5, 0.09375, ((0, 2), (1, 16)))
    segment = draw_segment(jax.random.fold_in(key_of[7], 71), 0)
    return {"hidden_in": hidden_in, "norm_gain": norm_gain, "w_query": w_query, "w_key": w_key, "w_value": w_value, "w_out": w_out, "segment": segment}


rope_theta = 500000.0
norm_epsilon = 1e-05

def inverse_frequency(head_width):
    exponent = jnp.arange(0, head_width, 2).astype(jnp.float32) / head_width
    base_freq = rope_theta ** (-exponent)
    wavelength = 2.0 * jnp.pi / base_freq
    smooth = (8192.0 / wavelength - 1.0) / 3.0
    blended = (1.0 - smooth) * base_freq / 8.0 + smooth * base_freq
    return jnp.where(wavelength < 2048.0, base_freq, jnp.where(wavelength > 8192.0, base_freq / 8.0, blended))

def positions_of(segment):
    row_index = jnp.arange(segment.shape[0], dtype=jnp.int32)
    changed = jnp.concatenate([jnp.ones((1,), dtype=bool), segment[1:] != segment[:-1]])
    begins = lax.cummax(jnp.where(changed, row_index, 0), axis=0)
    return row_index - begins

def rotate(vectors, position):
    head_width = vectors.shape[-1]
    half_width = head_width // 2
    angles = position.astype(jnp.float32)[:, None] * inverse_frequency(head_width)[None, :]
    cosine = jnp.concatenate([jnp.cos(angles), jnp.cos(angles)], axis=-1)[:, None, :]
    sine_table = jnp.concatenate([jnp.sin(angles), jnp.sin(angles)], axis=-1)[:, None, :]
    turned = jnp.concatenate([-vectors[..., half_width:], vectors[..., :half_width]], axis=-1)
    return vectors * cosine + turned * sine_table

def rms_normed(rows_float, norm_gain):
    mean_square = lax.optimization_barrier(jnp.mean(rows_float * rows_float, axis=-1, keepdims=True))
    return (rows_float * lax.rsqrt(mean_square + norm_epsilon) * norm_gain.astype(jnp.float32)).astype(jnp.bfloat16)

def visible_pairs(segment, first_key, key_count):
    row_index = jnp.arange(segment.shape[0], dtype=jnp.int32)
    key_index = first_key + jnp.arange(key_count, dtype=jnp.int32)
    key_segment = lax.dynamic_slice_in_dim(segment, first_key, key_count, 0)
    same_segment = (segment[:, None] == key_segment[None, :]) & (segment[:, None] >= 0)
    causal = key_index[None, :] <= row_index[:, None]
    return same_segment & causal | (key_index[None, :] == row_index[:, None])

def reference(hidden_in, norm_gain, w_query, w_key, w_value, w_out, segment):
    group_size = HQ // KVH
    score_scale = HEAD ** (-0.5)
    per_group = HQ * HEAD // N_TENSOR
    out_float = w_out.astype(jnp.float32).reshape(N_TENSOR, per_group, D)

    def one_pack(packed):
        row_block, pack_segment = packed
        rows_float = row_block.astype(jnp.float32)
        normed = rms_normed(rows_float, norm_gain)
        position = positions_of(pack_segment)
        query_raw = jnp.dot(normed, w_query, preferred_element_type=jnp.float32).reshape(PACK, HQ, HEAD)
        key_raw = jnp.dot(normed, w_key, preferred_element_type=jnp.float32).reshape(PACK, KVH, HEAD)
        value_raw = jnp.dot(normed, w_value, preferred_element_type=jnp.float32).reshape(PACK, KVH, HEAD)
        query_rows = rotate(query_raw, position).astype(jnp.bfloat16)
        key_rows = rotate(key_raw, position).astype(jnp.bfloat16)
        value_rows = value_raw.astype(jnp.bfloat16)
        cache_rows = jnp.concatenate([key_rows, value_rows], axis=-1)
        query_float = query_rows.astype(jnp.float32).reshape(PACK, KVH, group_size, HEAD)
        scores = jnp.einsum('skgh,tkh->kgst', query_float, key_rows.astype(jnp.float32)) * score_scale
        allowed = visible_pairs(pack_segment, 0, PACK)
        scores = jnp.where(allowed, scores, -jnp.inf)
        row_max = lax.optimization_barrier(jnp.max(scores, axis=-1, keepdims=True))
        weight = jnp.exp(scores - row_max)
        weight_sum = lax.optimization_barrier(jnp.sum(weight, axis=-1))
        weight_low = lax.optimization_barrier(weight.astype(jnp.bfloat16))
        mixed_rows = jnp.einsum('kgst,tkh->kgsh', weight_low.astype(jnp.float32), value_rows.astype(jnp.float32)) / weight_sum[..., None]
        attended = jnp.transpose(mixed_rows, (2, 0, 1, 3)).astype(jnp.bfloat16).reshape(PACK, HQ * HEAD)
        grouped = attended.astype(jnp.float32).reshape(PACK, N_TENSOR, per_group)
        partial_sums = jnp.einsum('sgc,gcd->gsd', grouped, out_float)
        partial_low = lax.optimization_barrier(partial_sums.astype(jnp.bfloat16))
        hidden_rows = (lax.optimization_barrier(jnp.sum(partial_low.astype(jnp.float32), axis=0)) + rows_float).astype(jnp.bfloat16)
        return (hidden_rows, cache_rows)
    hidden_out, cache_out = lax.map(one_pack, (hidden_in.reshape(N_DP, PACK, D), segment.reshape(N_DP, PACK)))
    return (hidden_out.reshape(PACK * N_DP, D), cache_out.reshape(PACK * N_DP, KVH, 2 * HEAD))
```

```python
import functools

import jax
import jax.numpy as jnp
from jax import lax
from jax.experimental import pallas as pl
from jax.experimental.pallas import tpu as pltpu
from jax.sharding import PartitionSpec as P

HEAD = 128


rope_theta = 500000.0
norm_epsilon = 1e-05


def inverse_frequency(head_width):
    exponent = jnp.arange(0, head_width, 2).astype(jnp.float32) / head_width
    base_freq = rope_theta ** (-exponent)
    wavelength = 2.0 * jnp.pi / base_freq
    smooth = (8192.0 / wavelength - 1.0) / 3.0
    blended = (1.0 - smooth) * base_freq / 8.0 + smooth * base_freq
    return jnp.where(
        wavelength < 2048.0, base_freq, jnp.where(wavelength > 8192.0, base_freq / 8.0, blended)
    )


def positions_of(segment):
    row_index = jnp.arange(segment.shape[0], dtype=jnp.int32)
    changed = jnp.concatenate([jnp.ones((1,), dtype=bool), segment[1:] != segment[:-1]])
    earlier = changed[None, :] & (row_index[None, :] <= row_index[:, None])
    return row_index - jnp.max(jnp.where(earlier, row_index[None, :], 0), axis=1)


def rotate(vectors, position):
    head_width = vectors.shape[-1]
    half_width = head_width // 2
    angles = position.astype(jnp.float32)[:, None] * inverse_frequency(head_width)[None, :]
    cosine = jnp.concatenate([jnp.cos(angles), jnp.cos(angles)], axis=-1)[:, None, :]
    sine_table = jnp.concatenate([jnp.sin(angles), jnp.sin(angles)], axis=-1)[:, None, :]
    turned = jnp.concatenate([-vectors[..., half_width:], vectors[..., :half_width]], axis=-1)
    return vectors * cosine + turned * sine_table


def rms_normed(rows_float, norm_gain):
    mean_square = jnp.mean(rows_float * rows_float, axis=-1, keepdims=True)
    return (
        rows_float * lax.rsqrt(mean_square + norm_epsilon) * norm_gain.astype(jnp.float32)
    ).astype(jnp.bfloat16)


def visible_pairs(segment, key_count):
    row_index = jnp.arange(segment.shape[0], dtype=jnp.int32)
    key_index = jnp.arange(key_count, dtype=jnp.int32)
    same_segment = (segment[:, None] == segment[None, :]) & (segment[:, None] >= 0)
    causal = key_index[None, :] <= row_index[:, None]
    return same_segment & causal | (key_index[None, :] == row_index[:, None])


def body(hidden_in, norm_gain, w_query, w_key, w_value, w_out, segment):
    pack_rows = segment.shape[0]
    query_cols = w_query.shape[1]
    kv_cols = w_key.shape[1]
    query_heads = query_cols // HEAD
    kv_heads = kv_cols // HEAD
    group_size = query_heads // kv_heads
    score_scale = HEAD ** (-0.5)
    rows_float = hidden_in.astype(jnp.float32)
    normed = rms_normed(rows_float, norm_gain)
    gathered = lax.all_gather(normed, "tensor", axis=0, tiled=True)
    joined = jnp.concatenate(
        (
            lax.all_gather(w_query, "dp", axis=0, tiled=True),
            lax.all_gather(w_key, "dp", axis=0, tiled=True),
            lax.all_gather(w_value, "dp", axis=0, tiled=True),
        ),
        axis=1,
    )
    projected = jnp.dot(gathered, joined, preferred_element_type=jnp.float32)
    position = positions_of(segment)
    query_rows = rotate(
        projected[:, :query_cols].reshape(pack_rows, query_heads, HEAD), position
    ).astype(jnp.bfloat16)
    key_rows = rotate(
        projected[:, query_cols : query_cols + kv_cols].reshape(pack_rows, kv_heads, HEAD), position
    ).astype(jnp.bfloat16)
    value_rows = (
        projected[:, query_cols + kv_cols :].astype(jnp.bfloat16).reshape(pack_rows, kv_heads, HEAD)
    )
    cache_rows = jnp.concatenate([key_rows, value_rows], axis=-1)
    grouped_query = query_rows.reshape(pack_rows, kv_heads, group_size, HEAD)
    scores = (
        jnp.einsum("skgh,tkh->kgst", grouped_query, key_rows, preferred_element_type=jnp.float32)
        * score_scale
    )
    allowed = visible_pairs(segment, pack_rows)
    scores = jnp.where(allowed, scores, -1e30)
    row_max = jnp.max(scores, axis=-1, keepdims=True)
    weight = jnp.exp(scores - row_max)
    weight_sum = jnp.sum(weight, axis=-1)
    mixed_rows = (
        jnp.einsum(
            "kgst,tkh->kgsh",
            weight.astype(jnp.bfloat16),
            value_rows,
            preferred_element_type=jnp.float32,
        )
        / weight_sum[..., None]
    )
    attended = (
        jnp.transpose(mixed_rows, (2, 0, 1, 3)).astype(jnp.bfloat16).reshape(pack_rows, query_cols)
    )
    out_full = lax.all_gather(w_out, "dp", axis=1, tiled=True)
    summed = lax.psum_scatter(
        jnp.dot(attended, out_full, preferred_element_type=jnp.float32).astype(jnp.bfloat16),
        "tensor",
        scatter_dimension=0,
        tiled=True,
    ).astype(jnp.float32)
    hidden_out = (summed + rows_float).astype(jnp.bfloat16)
    return (hidden_out, cache_rows)


MESH = pl.DeviceIdType.MESH


def fused_kernel(
    nz, hidden_ref, gain_ref, wj_ref, wo_ref, aux_ref,
    out_ref, cache_ref,
    act, w_buf, o_buf, aux_buf, acc, att, part, got, cache_send, cache_got,
    local_sem, x_send, x_recv, act_send, act_recv,
    w_send, w_recv, o_send, o_recv, sum_send, sum_recv,
):
    dp = lax.axis_index("dp")
    y = lax.axis_index("tensor")
    z = dp // 4
    x = (dp // 2) % 2
    c = dp % 2
    ox, oy, oc = 1 - x, 1 - y, 1 - c

    def dev(zz, xx, cc, yy):
        return {"dp": zz * 4 + xx * 2 + cc, "tensor": yy}

    x_peer = dev(z, ox, c, y)
    sibling = dev(z, x, oc, y)
    has_up = z + 1 < nz
    has_down = z > 0
    up = dev(jnp.minimum(z + 1, nz - 1), x, c, y)
    down = dev(jnp.maximum(z - 1, 0), x, c, y)
    trio = ((0, 1), (1, 0), (1, 1))

    def flip(delta):
        return (x + delta[0]) % 2, (y + delta[1]) % 2

    barrier = pltpu.get_barrier_semaphore()
    for delta in trio:
        px, py = flip(delta)
        pl.semaphore_signal(barrier, inc=1, device_id=dev(z, px, c, py), device_id_type=MESH)
    pl.semaphore_signal(barrier, inc=1, device_id=sibling, device_id_type=MESH)

    @pl.when(has_up)
    def _():
        pl.semaphore_signal(barrier, inc=1, device_id=up, device_id_type=MESH)

    @pl.when(has_down)
    def _():
        pl.semaphore_signal(barrier, inc=1, device_id=down, device_id_type=MESH)

    pl.semaphore_wait(barrier, 4 + jnp.where(has_up, 1, 0) + jnp.where(has_down, 1, 0))

    def remote(src, dst, send, recv, device):
        return pltpu.make_async_remote_copy(
            src_ref=src, dst_ref=dst, send_sem=send, recv_sem=recv, device_id=device, device_id_type=MESH
        )

    class Ring:
        def __init__(self, buf, src, send, recv, at):
            self.buf, self.src, self.send, self.recv, self.at = buf, src, send, recv, at

        def own(self, h):
            return pltpu.make_async_copy(
                self.src.at[x, h], self.buf.at[z, x, c, h], local_sem.at[self.at + h]
            )

        def cross(self, h):
            return remote(
                self.src.at[ox, h], self.buf.at[z, x, c, h],
                x_send.at[self.at + h], self.recv.at[z, x, c, h], x_peer,
            )

        def hop(self, way, zs, xs, h, device):
            slot = self.buf.at[zs, xs, c, h]
            return remote(slot, slot, self.send.at[way, zs, xs, h], self.recv.at[zs, xs, c, h], device)

        def arrived(self, zs, xs, cc, h):
            slot = self.buf.at[zs, xs, cc, h]
            remote(slot, slot, self.send.at[0, 0, 0, 0], self.recv.at[zs, xs, cc, h], sibling).wait_recv()

        def forward(self, d):
            def one(t, carry):
                xs = (x + t // 2) % 2
                h = t % 2
                if d == 0:
                    @pl.when(t >= 2)
                    def _():
                        self.arrived(z, xs, c, h)

                    @pl.when(has_up)
                    def _():
                        self.hop(0, z, xs, h, up).start()

                    @pl.when(has_down)
                    def _():
                        self.hop(1, z, xs, h, down).start()

                    self.hop(2, z, xs, h, sibling).start()
                else:
                    @pl.when(z - d >= 0)
                    def _():
                        zs = z - d
                        self.arrived(zs, xs, c, h)

                        @pl.when(has_up)
                        def _():
                            self.hop(0, zs, xs, h, up).start()

                        self.hop(2, zs, xs, h, sibling).start()

                    @pl.when(z + d < nz)
                    def _():
                        zs = z + d
                        self.arrived(zs, xs, c, h)

                        @pl.when(has_down)
                        def _():
                            self.hop(1, zs, xs, h, down).start()

                        self.hop(2, zs, xs, h, sibling).start()

                return carry

            lax.fori_loop(0, 4, one, 0)

        def sibling_part(self, zs):
            def one(t, carry):
                self.arrived(zs, (x + t // 2) % 2, oc, t % 2)
                return carry

            lax.fori_loop(0, 4, one, 0)

        def finish(self):
            for h in range(2):
                self.cross(h).wait_send()

            def one(t, carry):
                zs, xs, h = t // 4, (t // 2) % 2, t % 2

                @pl.when((zs <= z) & has_up)
                def _():
                    self.hop(0, zs, xs, h, up).wait_send()

                @pl.when((zs >= z) & has_down)
                def _():
                    self.hop(1, zs, xs, h, down).wait_send()

                self.hop(2, zs, xs, h, sibling).wait_send()
                return carry

            lax.fori_loop(0, nz * 4, one, 0)

    qkv = Ring(w_buf, wj_ref, w_send, w_recv, 0)
    outw = Ring(o_buf, wo_ref, o_send, o_recv, 2)

    for h in range(2):
        qkv.cross(h).start()
    for ring in (qkv, outw):
        for h in range(2):
            ring.own(h).start()

    rows = hidden_ref[...].astype(jnp.float32)
    mean_square = jnp.mean(rows * rows, axis=-1, keepdims=True)
    mine = x * 2 + y
    act[mine] = (rows * lax.rsqrt(mean_square + norm_epsilon) * gain_ref[...]).astype(jnp.bfloat16)
    aux_buf[x] = aux_ref[...]

    def act_copy(k):
        px, py = flip(trio[k])
        return remote(act.at[mine], act.at[mine], act_send.at[k], act_recv.at[mine], dev(z, px, c, py))

    for ring in (qkv, outw):
        for h in range(2):
            ring.own(h).wait()
    for k in range(3):
        act_copy(k).start()
    aux_copy = remote(aux_ref, aux_buf.at[x], x_send.at[4], x_recv.at[0], x_peer)
    aux_copy.start()
    qkv.forward(0)
    for h in range(2):
        outw.cross(h).start()
    for k in range(3):
        px, py = flip(trio[k])
        q = px * 2 + py
        remote(act.at[q], act.at[q], act_send.at[0], act_recv.at[q], sibling).wait_recv()

    rows_here = act.shape[0] * act.shape[1]
    span = act.shape[2] // nz
    width = acc.shape[1]
    acc[...] = jnp.zeros_like(acc)

    def project(zs):
        qkv.sibling_part(zs)
        cols = pl.ds(pl.multiple_of(zs * span, span), span)

        def one(n, carry):
            at = pl.ds(pl.multiple_of(n * 256, 256), 256)
            left = act[:, :, cols].reshape(rows_here, span)
            right = w_buf[zs, :, :, :, :, at].reshape(span, 256)
            acc[:, at] += jnp.dot(left, right, preferred_element_type=jnp.float32)
            return carry

        lax.fori_loop(0, width // 256, one, 0)

    def each(d, work):
        if d == 0:
            work(z)
        else:
            @pl.when(z - d >= 0)
            def _():
                work(z - d)

            @pl.when(z + d < nz)
            def _():
                work(z + d)

    for d in range(nz):
        if d:
            qkv.forward(d)
        if d == nz - 1:
            outw.forward(0)
        each(d, project)

    aux_copy.wait_send()
    remote(aux_ref, aux_buf.at[ox], x_send.at[4], x_recv.at[0], x_peer).wait_recv()
    lane = lax.broadcasted_iota(jnp.int32, (256, HEAD), 1)
    row_at = lax.broadcasted_iota(jnp.int32, (256, 256), 0)
    key_at = lax.broadcasted_iota(jnp.int32, (256, 256), 1)
    query_width = att.shape[1]
    kv_heads = (width - query_width) // (2 * HEAD)
    group = query_width // HEAD // kv_heads

    def attend(t, carry):
        p = (ox + t // kv_heads) % 2
        g = t % kv_heads
        table = aux_buf[p, 0:256, :]
        swapped = pltpu.roll(table, HEAD // 2, 1)
        cosine = jnp.where(lane < HEAD // 2, table, swapped)
        sine = jnp.where(lane < HEAD // 2, -swapped, table)
        seg = jnp.concatenate([aux_buf[p, 256:257, :], aux_buf[p, 257:258, :]], axis=1)
        seg_key = jnp.broadcast_to(seg, (256, 256))
        seg_row = seg_key.T
        allowed = ((seg_key == seg_row) & (seg_row >= 0) & (key_at <= row_at)) | (key_at == row_at)
        pack = pl.ds(pl.multiple_of(p * 256, 256), 256)

        def head_of(at):
            return acc[pack, pl.ds(pl.multiple_of(at * HEAD, HEAD), HEAD)]

        def turned(v):
            return (v * cosine + pltpu.roll(v, HEAD // 2, 1) * sine).astype(jnp.bfloat16)

        key = turned(head_of(query_width // HEAD + g))
        value = head_of(query_width // HEAD + kv_heads + g).astype(jnp.bfloat16)
        cache_send[p, :, pl.ds(pl.multiple_of(g * 256, 256), HEAD)] = key
        cache_send[p, :, pl.ds(pl.multiple_of(g * 256 + HEAD, HEAD), HEAD)] = value
        for i in range(group):
            query = turned(head_of(g * group + i))
            scores = lax.dot_general(
                query, key, (((1,), (1,)), ((), ())), preferred_element_type=jnp.float32
            ) * HEAD ** (-0.5)
            scores = jnp.where(allowed, scores, -1e30)
            weight = jnp.exp(scores - jnp.max(scores, axis=-1, keepdims=True))
            total = jnp.sum(weight, axis=-1, keepdims=True)
            mixed = jnp.dot(weight.astype(jnp.bfloat16), value, preferred_element_type=jnp.float32)
            att[pack, pl.ds(pl.multiple_of((g * group + i) * HEAD, HEAD), HEAD)] = (mixed / total).astype(
                jnp.bfloat16
            )
        return carry

    lax.fori_loop(0, 2 * kv_heads, attend, 0)
    cache_copy = remote(cache_send.at[ox], cache_got, x_send.at[5], x_recv.at[1], x_peer)
    cache_copy.start()

    def sum_copy(zs, k):
        px, py = flip(trio[k])
        return remote(
            part.at[zs, px * 2 + py], got.at[zs, k], sum_send.at[zs, k], sum_recv.at[zs, k],
            dev(z, px, c, py),
        )

    def outward(zs):
        outw.sibling_part(zs)
        depth = o_buf.shape[3] * o_buf.shape[4]
        cols = o_buf.shape[5]

        for n in range(4):
            right = o_buf[zs, n // 2, n % 2].reshape(depth, cols)
            product = jnp.dot(att[...], right, preferred_element_type=jnp.float32)
            part[zs, :, :, n * cols : (n + 1) * cols] = product.astype(jnp.bfloat16).reshape(
                4, rows_here // 4, cols
            )
        for k in (2, 1, 0):
            sum_copy(zs, k).start()

    for d in range(nz):
        if d:
            outw.forward(d)
        each(d, outward)

    cache_copy.wait()
    kept = cache_ref.shape[1] // 2
    cache_ref[:, pl.ds(pl.multiple_of(x * kept, kept), kept)] = cache_send[x]
    cache_ref[:, pl.ds(pl.multiple_of(ox * kept, kept), kept)] = cache_got[...]
    qkv.finish()
    outw.finish()
    for k in range(3):
        act_copy(k).wait_send()

    def settle(zs):
        for k in range(3):
            sum_copy(zs, k).wait()
        cols = pl.ds(pl.multiple_of(zs * span, span), span)
        total = part[zs, mine].astype(jnp.float32)
        for k in range(3):
            total = total + got[zs, k].astype(jnp.float32)
        out_ref[:, cols] = (total + hidden_ref[:, cols].astype(jnp.float32)).astype(jnp.bfloat16)

    for d in range(nz):
        each(d, settle)


def fused_body(n_dp, hidden_in, norm_gain, w_query, w_key, w_value, w_out, segment):
    nz = n_dp // 4
    rows, features = hidden_in.shape
    pack_rows = segment.shape[0]
    depth, query_cols = w_query.shape
    kv_cols = w_key.shape[1]
    width = (query_cols + 2 * kv_cols) // 2
    out_cols = w_out.shape[1]

    def halves(w):
        return jnp.transpose(w.reshape(depth, 2, w.shape[1] // 2), (1, 0, 2))

    joined = jnp.concatenate((halves(w_query), halves(w_key), halves(w_value)), axis=2)
    joined = joined.reshape(2, 2, depth // 2, width)
    out_parts = w_out.reshape(2, 2, query_cols // 4, out_cols)
    angles = positions_of(segment).astype(jnp.float32)[:, None] * inverse_frequency(HEAD)[None, :]
    aux = jnp.concatenate(
        (
            jnp.cos(angles), jnp.sin(angles),
        ),
        axis=1,
    )
    aux = jnp.concatenate(
        (aux, segment.astype(jnp.float32).reshape(pack_rows // 128, 128), jnp.zeros((6, 128), jnp.float32)), axis=0
    )
    vmem = pl.BlockSpec(memory_space=pltpu.VMEM)
    dma = pltpu.SemaphoreType.DMA
    low = jnp.bfloat16
    hidden_out, cache = pl.pallas_call(
        functools.partial(fused_kernel, nz),
        out_shape=(
            jax.ShapeDtypeStruct((rows, features), low),
            jax.ShapeDtypeStruct((pack_rows, 2 * kv_cols), low),
        ),
        in_specs=[vmem] * 5,
        out_specs=(vmem, vmem),
        scratch_shapes=[
            pltpu.VMEM((4, rows, features), low),
            pltpu.VMEM((nz, 2, 2, 2, depth // 2, width), low),
            pltpu.VMEM((nz, 2, 2, 2, query_cols // 4, out_cols), low),
            pltpu.VMEM((2,) + aux.shape, jnp.float32),
            pltpu.VMEM((4 * rows, width), jnp.float32),
            pltpu.VMEM((4 * rows, query_cols // 2), low),
            pltpu.VMEM((nz, 4, rows, features // nz), low),
            pltpu.VMEM((nz, 3, rows, features // nz), low),
            pltpu.VMEM((2, pack_rows, kv_cols), low),
            pltpu.VMEM((pack_rows, kv_cols), low),
            dma((4,)), dma((6,)), dma((2,)), dma((3,)), dma((4,)),
            dma((3, nz, 2, 2)), dma((nz, 2, 2, 2)), dma((3, nz, 2, 2)), dma((nz, 2, 2, 2)),
            dma((nz, 3)), dma((nz, 3)),
        ],
        compiler_params=pltpu.CompilerParams(
            collective_id=0, has_side_effects=True, vmem_limit_bytes=60 * 1024 * 1024
        ),
    )(hidden_in, norm_gain.astype(jnp.float32).reshape(1, features), joined, out_parts, aux)
    return hidden_out, cache.reshape(pack_rows, kv_cols // HEAD, 2 * HEAD)


def solution(mesh):
    n_dp, n_tensor = mesh.shape["dp"], mesh.shape["tensor"]

    def chosen(*blocks):
        if n_tensor == 2 and n_dp % 4 == 0 and (blocks[3].shape[1] // HEAD) % 2 == 0:
            return fused_body(n_dp, *blocks)
        return body(*blocks)

    return jax.shard_map(
        chosen,
        mesh=mesh,
        in_specs=(
            P(("dp", "tensor"), None),
            P(),
            P("dp", "tensor"),
            P("dp", "tensor"),
            P("dp", "tensor"),
            P("tensor", "dp"),
            P("dp"),
        ),
        out_specs=(P(("dp", "tensor"), None), P("dp", "tensor", None)),
        check_vma=False,
    )
```

```python
import functools

import jax
import jax.numpy as jnp
from jax import lax
from jax.experimental import pallas as pl
from jax.experimental.pallas import tpu as pltpu
from jax.sharding import PartitionSpec as P

HEAD = 128


rope_theta = 500000.0
norm_epsilon = 1e-05


def inverse_frequency(head_width):
    exponent = jnp.arange(0, head_width, 2).astype(jnp.float32) / head_width
    base_freq = rope_theta ** (-exponent)
    wavelength = 2.0 * jnp.pi / base_freq
    smooth = (8192.0 / wavelength - 1.0) / 3.0
    blended = (1.0 - smooth) * base_freq / 8.0 + smooth * base_freq
    return jnp.where(
        wavelength < 2048.0, base_freq, jnp.where(wavelength > 8192.0, base_freq / 8.0, blended)
    )


def positions_of(segment):
    row_index = jnp.arange(segment.shape[0], dtype=jnp.int32)
    changed = jnp.concatenate([jnp.ones((1,), dtype=bool), segment[1:] != segment[:-1]])
    earlier = changed[None, :] & (row_index[None, :] <= row_index[:, None])
    return row_index - jnp.max(jnp.where(earlier, row_index[None, :], 0), axis=1)


def rotate(vectors, position):
    head_width = vectors.shape[-1]
    half_width = head_width // 2
    angles = position.astype(jnp.float32)[:, None] * inverse_frequency(head_width)[None, :]
    cosine = jnp.concatenate([jnp.cos(angles), jnp.cos(angles)], axis=-1)[:, None, :]
    sine_table = jnp.concatenate([jnp.sin(angles), jnp.sin(angles)], axis=-1)[:, None, :]
    turned = jnp.concatenate([-vectors[..., half_width:], vectors[..., :half_width]], axis=-1)
    return vectors * cosine + turned * sine_table


def rms_normed(rows_float, norm_gain):
    mean_square = jnp.mean(rows_float * rows_float, axis=-1, keepdims=True)
    return (
        rows_float * lax.rsqrt(mean_square + norm_epsilon) * norm_gain.astype(jnp.float32)
    ).astype(jnp.bfloat16)


def visible_pairs(segment, key_count):
    row_index = jnp.arange(segment.shape[0], dtype=jnp.int32)
    key_index = jnp.arange(key_count, dtype=jnp.int32)
    same_segment = (segment[:, None] == segment[None, :]) & (segment[:, None] >= 0)
    causal = key_index[None, :] <= row_index[:, None]
    return same_segment & causal | (key_index[None, :] == row_index[:, None])


def body(hidden_in, norm_gain, w_query, w_key, w_value, w_out, segment):
    pack_rows = segment.shape[0]
    query_cols = w_query.shape[1]
    kv_cols = w_key.shape[1]
    query_heads = query_cols // HEAD
    kv_heads = kv_cols // HEAD
    group_size = query_heads // kv_heads
    score_scale = HEAD ** (-0.5)
    rows_float = hidden_in.astype(jnp.float32)
    normed = rms_normed(rows_float, norm_gain)
    gathered = lax.all_gather(normed, "tensor", axis=0, tiled=True)
    joined = jnp.concatenate(
        (
            lax.all_gather(w_query, "dp", axis=0, tiled=True),
            lax.all_gather(w_key, "dp", axis=0, tiled=True),
            lax.all_gather(w_value, "dp", axis=0, tiled=True),
        ),
        axis=1,
    )
    projected = jnp.dot(gathered, joined, preferred_element_type=jnp.float32)
    position = positions_of(segment)
    query_rows = rotate(
        projected[:, :query_cols].reshape(pack_rows, query_heads, HEAD), position
    ).astype(jnp.bfloat16)
    key_rows = rotate(
        projected[:, query_cols : query_cols + kv_cols].reshape(pack_rows, kv_heads, HEAD), position
    ).astype(jnp.bfloat16)
    value_rows = (
        projected[:, query_cols + kv_cols :].astype(jnp.bfloat16).reshape(pack_rows, kv_heads, HEAD)
    )
    cache_rows = jnp.concatenate([key_rows, value_rows], axis=-1)
    grouped_query = query_rows.reshape(pack_rows, kv_heads, group_size, HEAD)
    scores = (
        jnp.einsum("skgh,tkh->kgst", grouped_query, key_rows, preferred_element_type=jnp.float32)
        * score_scale
    )
    allowed = visible_pairs(segment, pack_rows)
    scores = jnp.where(allowed, scores, -1e30)
    row_max = jnp.max(scores, axis=-1, keepdims=True)
    weight = jnp.exp(scores - row_max)
    weight_sum = jnp.sum(weight, axis=-1)
    mixed_rows = (
        jnp.einsum(
            "kgst,tkh->kgsh",
            weight.astype(jnp.bfloat16),
            value_rows,
            preferred_element_type=jnp.float32,
        )
        / weight_sum[..., None]
    )
    attended = (
        jnp.transpose(mixed_rows, (2, 0, 1, 3)).astype(jnp.bfloat16).reshape(pack_rows, query_cols)
    )
    out_full = lax.all_gather(w_out, "dp", axis=1, tiled=True)
    summed = lax.psum_scatter(
        jnp.dot(attended, out_full, preferred_element_type=jnp.float32).astype(jnp.bfloat16),
        "tensor",
        scatter_dimension=0,
        tiled=True,
    ).astype(jnp.float32)
    hidden_out = (summed + rows_float).astype(jnp.bfloat16)
    return (hidden_out, cache_rows)


MESH = pl.DeviceIdType.MESH


def fused_kernel(
    nz, hidden_ref, gain_ref, wj_ref, wo_ref, aux_ref,
    out_ref, cache_ref,
    act, w_buf, o_buf, aux_buf, acc, att, part, got, cache_send, cache_got,
    local_sem, x_send, x_recv, act_send, act_recv,
    w_send, w_recv, o_send, o_recv, sum_send, sum_recv,
):
    dp = lax.axis_index("dp")
    y = lax.axis_index("tensor")
    z = dp // 4
    x = (dp // 2) % 2
    c = dp % 2
    ox, oy, oc = 1 - x, 1 - y, 1 - c

    def dev(zz, xx, cc, yy):
        return {"dp": zz * 4 + xx * 2 + cc, "tensor": yy}

    x_peer = dev(z, ox, c, y)
    sibling = dev(z, x, oc, y)
    has_up = z + 1 < nz
    has_down = z > 0
    up = dev(jnp.minimum(z + 1, nz - 1), x, c, y)
    down = dev(jnp.maximum(z - 1, 0), x, c, y)
    trio = ((0, 1), (1, 0), (1, 1))

    def flip(delta):
        return (x + delta[0]) % 2, (y + delta[1]) % 2

    barrier = pltpu.get_barrier_semaphore()
    for delta in trio:
        px, py = flip(delta)
        pl.semaphore_signal(barrier, inc=1, device_id=dev(z, px, c, py), device_id_type=MESH)
    pl.semaphore_signal(barrier, inc=1, device_id=sibling, device_id_type=MESH)

    @pl.when(has_up)
    def _():
        pl.semaphore_signal(barrier, inc=1, device_id=up, device_id_type=MESH)

    @pl.when(has_down)
    def _():
        pl.semaphore_signal(barrier, inc=1, device_id=down, device_id_type=MESH)

    pl.semaphore_wait(barrier, 4 + jnp.where(has_up, 1, 0) + jnp.where(has_down, 1, 0))

    def remote(src, dst, send, recv, device):
        return pltpu.make_async_remote_copy(
            src_ref=src, dst_ref=dst, send_sem=send, recv_sem=recv, device_id=device, device_id_type=MESH
        )

    class Ring:
        def __init__(self, buf, src, send, recv, at):
            self.buf, self.src, self.send, self.recv, self.at = buf, src, send, recv, at

        def own(self, h):
            return pltpu.make_async_copy(
                self.src.at[x, h], self.buf.at[z, x, c, h], local_sem.at[self.at + h]
            )

        def cross(self, h):
            return remote(
                self.src.at[ox, h], self.buf.at[z, x, c, h],
                x_send.at[self.at + h], self.recv.at[z, x, c, h], x_peer,
            )

        def hop(self, way, zs, xs, h, device):
            slot = self.buf.at[zs, xs, c, h]
            return remote(slot, slot, self.send.at[way, zs, xs, h], self.recv.at[zs, xs, c, h], device)

        def arrived(self, zs, xs, cc, h):
            slot = self.buf.at[zs, xs, cc, h]
            remote(slot, slot, self.send.at[0, 0, 0, 0], self.recv.at[zs, xs, cc, h], sibling).wait_recv()

        def forward(self, d, work=None, first=0, last=4):
            def one(t, carry):
                xs = (x + t // 2) % 2
                h = t % 2
                if d == 0:
                    @pl.when(t >= 2)
                    def _():
                        self.arrived(z, xs, c, h)

                    @pl.when(has_up)
                    def _():
                        self.hop(0, z, xs, h, up).start()

                    @pl.when(has_down)
                    def _():
                        self.hop(1, z, xs, h, down).start()

                    self.hop(2, z, xs, h, sibling).start()
                else:
                    @pl.when(z - d >= 0)
                    def _():
                        zs = z - d
                        self.arrived(zs, xs, c, h)

                        @pl.when(has_up)
                        def _():
                            self.hop(0, zs, xs, h, up).start()

                        self.hop(2, zs, xs, h, sibling).start()

                    @pl.when(z + d < nz)
                    def _():
                        zs = z + d
                        self.arrived(zs, xs, c, h)

                        @pl.when(has_down)
                        def _():
                            self.hop(1, zs, xs, h, down).start()

                        self.hop(2, zs, xs, h, sibling).start()

                if work is not None:
                    work(t)
                return carry

            lax.fori_loop(first, last, one, 0)

        def sibling_part(self, zs):
            def one(t, carry):
                self.arrived(zs, (x + t // 2) % 2, oc, t % 2)
                return carry

            lax.fori_loop(0, 4, one, 0)

        def finish(self):
            for h in range(2):
                self.cross(h).wait_send()

            def one(t, carry):
                zs, xs, h = t // 4, (t // 2) % 2, t % 2

                @pl.when((zs <= z) & has_up)
                def _():
                    self.hop(0, zs, xs, h, up).wait_send()

                @pl.when((zs >= z) & has_down)
                def _():
                    self.hop(1, zs, xs, h, down).wait_send()

                self.hop(2, zs, xs, h, sibling).wait_send()
                return carry

            lax.fori_loop(0, nz * 4, one, 0)

    qkv = Ring(w_buf, wj_ref, w_send, w_recv, 0)
    outw = Ring(o_buf, wo_ref, o_send, o_recv, 2)

    for h in range(2):
        qkv.cross(h).start()
    for ring in (qkv, outw):
        for h in range(2):
            ring.own(h).start()
    for h in range(2):
        qkv.own(h).wait()
    qkv.forward(0, last=2)

    rows = hidden_ref[...].astype(jnp.float32)
    mean_square = jnp.mean(rows * rows, axis=-1, keepdims=True)
    mine = x * 2 + y
    act[mine] = (rows * lax.rsqrt(mean_square + norm_epsilon) * gain_ref[...]).astype(jnp.bfloat16)
    aux_buf[x] = aux_ref[...]

    def act_copy(k):
        px, py = flip(trio[k])
        return remote(act.at[mine], act.at[mine], act_send.at[k], act_recv.at[mine], dev(z, px, c, py))

    for k in range(3):
        act_copy(k).start()
    aux_copy = remote(aux_ref, aux_buf.at[x], x_send.at[4], x_recv.at[0], x_peer)
    aux_copy.start()
    qkv.forward(0, first=2)
    for h in range(2):
        outw.own(h).wait()

    rows_here = act.shape[0] * act.shape[1]
    span = act.shape[2] // nz
    width = acc.shape[1]
    acc[...] = jnp.zeros_like(acc)

    chunks = width // 256

    def project(zs, t):
        cols = pl.ds(pl.multiple_of(zs * span, span), span)

        def one(n, carry):
            at = pl.ds(pl.multiple_of(n * 256, 256), 256)
            left = act[:, :, cols].reshape(rows_here, span)
            right = w_buf[zs, :, :, :, :, at].reshape(span, 256)
            acc[:, at] += jnp.dot(left, right, preferred_element_type=jnp.float32)
            return carry

        @pl.when(t == 0)
        def _():
            qkv.sibling_part(zs)

        lax.fori_loop(t * chunks // 4, (t + 1) * chunks // 4, one, 0)

    def each(d, work):
        if d == 0:
            work(z)
        else:
            @pl.when(z - d >= 0)
            def _():
                work(z - d)

            @pl.when(z + d < nz)
            def _():
                work(z + d)

    def part_of(d, work):
        return lambda t: each(d, lambda zs: work(zs, t))

    def whole_of(d, work):
        def one(t, carry):
            part_of(d, work)(t)
            return carry

        lax.fori_loop(0, 4, one, 0)

    qkv.forward(1)
    for k in range(3):
        px, py = flip(trio[k])
        q = px * 2 + py
        remote(act.at[q], act.at[q], act_send.at[0], act_recv.at[q], sibling).wait_recv()
    for h in range(2):
        outw.cross(h).start()
    for d in range(2, nz):
        qkv.forward(d, part_of(d - 2, project))
    outw.forward(0)
    for d in range(nz - 2, nz):
        whole_of(d, project)

    aux_copy.wait_send()
    remote(aux_ref, aux_buf.at[ox], x_send.at[4], x_recv.at[0], x_peer).wait_recv()
    lane = lax.broadcasted_iota(jnp.int32, (256, HEAD), 1)
    row_at = lax.broadcasted_iota(jnp.int32, (256, 256), 0)
    key_at = lax.broadcasted_iota(jnp.int32, (256, 256), 1)
    query_width = att.shape[1]
    kv_heads = (width - query_width) // (2 * HEAD)
    group = query_width // HEAD // kv_heads

    def attend(t):
        p = (ox + t // kv_heads) % 2
        g = t % kv_heads
        table = aux_buf[p, 0:256, :]
        swapped = pltpu.roll(table, HEAD // 2, 1)
        cosine = jnp.where(lane < HEAD // 2, table, swapped)
        sine = jnp.where(lane < HEAD // 2, -swapped, table)
        seg = jnp.concatenate([aux_buf[p, 256:257, :], aux_buf[p, 257:258, :]], axis=1)
        seg_key = jnp.broadcast_to(seg, (256, 256))
        seg_row = seg_key.T
        allowed = ((seg_key == seg_row) & (seg_row >= 0) & (key_at <= row_at)) | (key_at == row_at)
        pack = pl.ds(pl.multiple_of(p * 256, 256), 256)

        def head_of(at):
            return acc[pack, pl.ds(pl.multiple_of(at * HEAD, HEAD), HEAD)]

        def turned(v):
            return (v * cosine + pltpu.roll(v, HEAD // 2, 1) * sine).astype(jnp.bfloat16)

        key = turned(head_of(query_width // HEAD + g))
        value = head_of(query_width // HEAD + kv_heads + g).astype(jnp.bfloat16)
        cache_send[p, :, pl.ds(pl.multiple_of(g * 256, 256), HEAD)] = key
        cache_send[p, :, pl.ds(pl.multiple_of(g * 256 + HEAD, HEAD), HEAD)] = value
        for i in range(group):
            query = turned(head_of(g * group + i))
            scores = lax.dot_general(
                query, key, (((1,), (1,)), ((), ())), preferred_element_type=jnp.float32
            ) * HEAD ** (-0.5)
            scores = jnp.where(allowed, scores, -1e30)
            weight = jnp.exp(scores - jnp.max(scores, axis=-1, keepdims=True))
            total = jnp.sum(weight, axis=-1, keepdims=True)
            mixed = jnp.dot(weight.astype(jnp.bfloat16), value, preferred_element_type=jnp.float32)
            att[pack, pl.ds(pl.multiple_of((g * group + i) * HEAD, HEAD), HEAD)] = (mixed / total).astype(
                jnp.bfloat16
            )

    outw.forward(1, attend)
    cache_copy = remote(cache_send.at[ox], cache_got, x_send.at[5], x_recv.at[1], x_peer)
    cache_copy.start()

    depth, cols_out = o_buf.shape[3] * o_buf.shape[4], o_buf.shape[5]

    def strip(n):
        return pl.ds(pl.multiple_of(n * cols_out, cols_out), cols_out)

    def sum_copy(zs, n, k):
        px, py = flip(trio[k])
        return remote(
            part.at[zs, px * 2 + py, :, strip(n)], got.at[zs, k, :, strip(n)],
            sum_send.at[zs, n, k], sum_recv.at[zs, n, k], dev(z, px, c, py),
        )

    def outward(zs, n):
        xs, cs = n // 2, n % 2

        @pl.when(cs == oc)
        def _():
            for h in range(2):
                outw.arrived(zs, xs, oc, h)

        right = o_buf[zs, xs, cs].reshape(depth, cols_out)
        product = jnp.dot(att[...], right, preferred_element_type=jnp.float32)
        part[zs, :, :, strip(n)] = product.astype(jnp.bfloat16).reshape(4, rows_here // 4, cols_out)
        for k in (2, 1, 0):
            sum_copy(zs, n, k).start()

    for d in range(2, nz):
        early = part_of(d - 2, outward)
        if d < nz - 1:
            outw.forward(d, early)
        else:
            late = part_of(d - 1, outward)

            def both(t):
                early(t)
                late(t)

            outw.forward(d, both)
    whole_of(nz - 1, outward)

    cache_copy.wait()
    kept = cache_ref.shape[1] // 2
    cache_ref[:, pl.ds(pl.multiple_of(x * kept, kept), kept)] = cache_send[x]
    cache_ref[:, pl.ds(pl.multiple_of(ox * kept, kept), kept)] = cache_got[...]
    qkv.finish()
    outw.finish()
    for k in range(3):
        act_copy(k).wait_send()

    def settle(zs):
        for n in range(4):
            for k in range(3):
                sum_copy(zs, n, k).wait()
        cols = pl.ds(pl.multiple_of(zs * span, span), span)
        total = part[zs, mine].astype(jnp.float32)
        for k in range(3):
            total = total + got[zs, k].astype(jnp.float32)
        out_ref[:, cols] = (total + hidden_ref[:, cols].astype(jnp.float32)).astype(jnp.bfloat16)

    for d in range(nz):
        each(d, settle)


def fused_body(n_dp, hidden_in, norm_gain, w_query, w_key, w_value, w_out, segment):
    nz = n_dp // 4
    rows, features = hidden_in.shape
    pack_rows = segment.shape[0]
    depth, query_cols = w_query.shape
    kv_cols = w_key.shape[1]
    width = (query_cols + 2 * kv_cols) // 2
    out_cols = w_out.shape[1]

    def halves(w):
        return jnp.transpose(w.reshape(depth, 2, w.shape[1] // 2), (1, 0, 2))

    joined = jnp.concatenate((halves(w_query), halves(w_key), halves(w_value)), axis=2)
    joined = joined.reshape(2, 2, depth // 2, width)
    out_parts = w_out.reshape(2, 2, query_cols // 4, out_cols)
    angles = positions_of(segment).astype(jnp.float32)[:, None] * inverse_frequency(HEAD)[None, :]
    aux = jnp.concatenate(
        (
            jnp.cos(angles), jnp.sin(angles),
        ),
        axis=1,
    )
    aux = jnp.concatenate(
        (aux, segment.astype(jnp.float32).reshape(pack_rows // 128, 128), jnp.zeros((6, 128), jnp.float32)), axis=0
    )
    vmem = pl.BlockSpec(memory_space=pltpu.VMEM)
    dma = pltpu.SemaphoreType.DMA
    low = jnp.bfloat16
    hidden_out, cache = pl.pallas_call(
        functools.partial(fused_kernel, nz),
        out_shape=(
            jax.ShapeDtypeStruct((rows, features), low),
            jax.ShapeDtypeStruct((pack_rows, 2 * kv_cols), low),
        ),
        in_specs=[vmem] * 5,
        out_specs=(vmem, vmem),
        scratch_shapes=[
            pltpu.VMEM((4, rows, features), low),
            pltpu.VMEM((nz, 2, 2, 2, depth // 2, width), low),
            pltpu.VMEM((nz, 2, 2, 2, query_cols // 4, out_cols), low),
            pltpu.VMEM((2,) + aux.shape, jnp.float32),
            pltpu.VMEM((4 * rows, width), jnp.float32),
            pltpu.VMEM((4 * rows, query_cols // 2), low),
            pltpu.VMEM((nz, 4, rows, features // nz), low),
            pltpu.VMEM((nz, 3, rows, features // nz), low),
            pltpu.VMEM((2, pack_rows, kv_cols), low),
            pltpu.VMEM((pack_rows, kv_cols), low),
            dma((4,)), dma((6,)), dma((2,)), dma((3,)), dma((4,)),
            dma((3, nz, 2, 2)), dma((nz, 2, 2, 2)), dma((3, nz, 2, 2)), dma((nz, 2, 2, 2)),
            dma((nz, 4, 3)), dma((nz, 4, 3)),
        ],
        compiler_params=pltpu.CompilerParams(
            collective_id=0, has_side_effects=True, vmem_limit_bytes=60 * 1024 * 1024
        ),
    )(hidden_in, norm_gain.astype(jnp.float32).reshape(1, features), joined, out_parts, aux)
    return hidden_out, cache.reshape(pack_rows, kv_cols // HEAD, 2 * HEAD)


def solution(mesh):
    n_dp, n_tensor = mesh.shape["dp"], mesh.shape["tensor"]

    def chosen(*blocks):
        if n_tensor == 2 and n_dp % 4 == 0 and n_dp >= 12 and blocks[3].shape[1] == 4 * HEAD:
            return fused_body(n_dp, *blocks)
        return body(*blocks)

    return jax.shard_map(
        chosen,
        mesh=mesh,
        in_specs=(
            P(("dp", "tensor"), None),
            P(),
            P("dp", "tensor"),
            P("dp", "tensor"),
            P("dp", "tensor"),
            P("tensor", "dp"),
            P("dp"),
        ),
        out_specs=(P(("dp", "tensor"), None), P("dp", "tensor", None)),
        check_vma=False,
    )
```

```python
import functools

import jax
import jax.numpy as jnp
from jax import lax
from jax.experimental import pallas as pl
from jax.experimental.pallas import tpu as pltpu
from jax.sharding import PartitionSpec as P

HEAD = 128


rope_theta = 500000.0
norm_epsilon = 1e-05


def inverse_frequency(head_width):
    exponent = jnp.arange(0, head_width, 2).astype(jnp.float32) / head_width
    base_freq = rope_theta ** (-exponent)
    wavelength = 2.0 * jnp.pi / base_freq
    smooth = (8192.0 / wavelength - 1.0) / 3.0
    blended = (1.0 - smooth) * base_freq / 8.0 + smooth * base_freq
    return jnp.where(
        wavelength < 2048.0, base_freq, jnp.where(wavelength > 8192.0, base_freq / 8.0, blended)
    )


def positions_of(segment):
    row_index = jnp.arange(segment.shape[0], dtype=jnp.int32)
    changed = jnp.concatenate([jnp.ones((1,), dtype=bool), segment[1:] != segment[:-1]])
    earlier = changed[None, :] & (row_index[None, :] <= row_index[:, None])
    return row_index - jnp.max(jnp.where(earlier, row_index[None, :], 0), axis=1)


def rotate(vectors, position):
    head_width = vectors.shape[-1]
    half_width = head_width // 2
    angles = position.astype(jnp.float32)[:, None] * inverse_frequency(head_width)[None, :]
    cosine = jnp.concatenate([jnp.cos(angles), jnp.cos(angles)], axis=-1)[:, None, :]
    sine_table = jnp.concatenate([jnp.sin(angles), jnp.sin(angles)], axis=-1)[:, None, :]
    turned = jnp.concatenate([-vectors[..., half_width:], vectors[..., :half_width]], axis=-1)
    return vectors * cosine + turned * sine_table


def rms_normed(rows_float, norm_gain):
    mean_square = jnp.mean(rows_float * rows_float, axis=-1, keepdims=True)
    return (
        rows_float * lax.rsqrt(mean_square + norm_epsilon) * norm_gain.astype(jnp.float32)
    ).astype(jnp.bfloat16)


def visible_pairs(segment, key_count):
    row_index = jnp.arange(segment.shape[0], dtype=jnp.int32)
    key_index = jnp.arange(key_count, dtype=jnp.int32)
    same_segment = (segment[:, None] == segment[None, :]) & (segment[:, None] >= 0)
    causal = key_index[None, :] <= row_index[:, None]
    return same_segment & causal | (key_index[None, :] == row_index[:, None])


def body(hidden_in, norm_gain, w_query, w_key, w_value, w_out, segment):
    pack_rows = segment.shape[0]
    query_cols = w_query.shape[1]
    kv_cols = w_key.shape[1]
    query_heads = query_cols // HEAD
    kv_heads = kv_cols // HEAD
    group_size = query_heads // kv_heads
    score_scale = HEAD ** (-0.5)
    rows_float = hidden_in.astype(jnp.float32)
    normed = rms_normed(rows_float, norm_gain)
    gathered = lax.all_gather(normed, "tensor", axis=0, tiled=True)
    joined = jnp.concatenate(
        (
            lax.all_gather(w_query, "dp", axis=0, tiled=True),
            lax.all_gather(w_key, "dp", axis=0, tiled=True),
            lax.all_gather(w_value, "dp", axis=0, tiled=True),
        ),
        axis=1,
    )
    projected = jnp.dot(gathered, joined, preferred_element_type=jnp.float32)
    position = positions_of(segment)
    query_rows = rotate(
        projected[:, :query_cols].reshape(pack_rows, query_heads, HEAD), position
    ).astype(jnp.bfloat16)
    key_rows = rotate(
        projected[:, query_cols : query_cols + kv_cols].reshape(pack_rows, kv_heads, HEAD), position
    ).astype(jnp.bfloat16)
    value_rows = (
        projected[:, query_cols + kv_cols :].astype(jnp.bfloat16).reshape(pack_rows, kv_heads, HEAD)
    )
    cache_rows = jnp.concatenate([key_rows, value_rows], axis=-1)
    grouped_query = query_rows.reshape(pack_rows, kv_heads, group_size, HEAD)
    scores = (
        jnp.einsum("skgh,tkh->kgst", grouped_query, key_rows, preferred_element_type=jnp.float32)
        * score_scale
    )
    allowed = visible_pairs(segment, pack_rows)
    scores = jnp.where(allowed, scores, -1e30)
    row_max = jnp.max(scores, axis=-1, keepdims=True)
    weight = jnp.exp(scores - row_max)
    weight_sum = jnp.sum(weight, axis=-1)
    mixed_rows = (
        jnp.einsum(
            "kgst,tkh->kgsh",
            weight.astype(jnp.bfloat16),
            value_rows,
            preferred_element_type=jnp.float32,
        )
        / weight_sum[..., None]
    )
    attended = (
        jnp.transpose(mixed_rows, (2, 0, 1, 3)).astype(jnp.bfloat16).reshape(pack_rows, query_cols)
    )
    out_full = lax.all_gather(w_out, "dp", axis=1, tiled=True)
    summed = lax.psum_scatter(
        jnp.dot(attended, out_full, preferred_element_type=jnp.float32).astype(jnp.bfloat16),
        "tensor",
        scatter_dimension=0,
        tiled=True,
    ).astype(jnp.float32)
    hidden_out = (summed + rows_float).astype(jnp.bfloat16)
    return (hidden_out, cache_rows)


MESH = pl.DeviceIdType.MESH


def fused_kernel(
    nz, hidden_ref, gain_ref, wj_ref, wo_ref, aux_ref,
    out_ref, cache_ref,
    act, w_buf, o_buf, aux_buf, acc, att, part, got, cache_send, cache_got,
    local_sem, x_send, x_recv, act_send, act_recv,
    w_send, w_recv, o_send, o_recv, sum_send, sum_recv,
):
    dp = lax.axis_index("dp")
    y = lax.axis_index("tensor")
    z = dp // 4
    x = (dp // 2) % 2
    c = dp % 2
    ox, oy, oc = 1 - x, 1 - y, 1 - c

    def dev(zz, xx, cc, yy):
        return {"dp": zz * 4 + xx * 2 + cc, "tensor": yy}

    x_peer = dev(z, ox, c, y)
    sibling = dev(z, x, oc, y)
    has_up = z + 1 < nz
    has_down = z > 0
    up = dev(jnp.minimum(z + 1, nz - 1), x, c, y)
    down = dev(jnp.maximum(z - 1, 0), x, c, y)
    trio = ((0, 1), (1, 0), (1, 1))

    def flip(delta):
        return (x + delta[0]) % 2, (y + delta[1]) % 2

    barrier = pltpu.get_barrier_semaphore()
    for delta in trio:
        px, py = flip(delta)
        pl.semaphore_signal(barrier, inc=1, device_id=dev(z, px, c, py), device_id_type=MESH)
    pl.semaphore_signal(barrier, inc=1, device_id=sibling, device_id_type=MESH)

    @pl.when(has_up)
    def _():
        pl.semaphore_signal(barrier, inc=1, device_id=up, device_id_type=MESH)

    @pl.when(has_down)
    def _():
        pl.semaphore_signal(barrier, inc=1, device_id=down, device_id_type=MESH)

    pl.semaphore_wait(barrier, 4 + jnp.where(has_up, 1, 0) + jnp.where(has_down, 1, 0))

    def remote(src, dst, send, recv, device):
        return pltpu.make_async_remote_copy(
            src_ref=src, dst_ref=dst, send_sem=send, recv_sem=recv, device_id=device, device_id_type=MESH
        )

    class Ring:
        def __init__(self, buf, src, send, recv, at):
            self.buf, self.src, self.send, self.recv, self.at = buf, src, send, recv, at

        def own(self, h):
            return pltpu.make_async_copy(
                self.src.at[x, h], self.buf.at[z, x, c, h], local_sem.at[self.at + h]
            )

        def cross(self, h):
            return remote(
                self.src.at[ox, h], self.buf.at[z, x, c, h],
                x_send.at[self.at + h], self.recv.at[z, x, c, h], x_peer,
            )

        def hop(self, way, zs, xs, h, device):
            slot = self.buf.at[zs, xs, c, h]
            return remote(slot, slot, self.send.at[way, zs, xs, h], self.recv.at[zs, xs, c, h], device)

        def arrived(self, zs, xs, cc, h):
            slot = self.buf.at[zs, xs, cc, h]
            remote(slot, slot, self.send.at[0, 0, 0, 0], self.recv.at[zs, xs, cc, h], sibling).wait_recv()

        def forward(self, d, work=None, first=0, last=4):
            def one(t, carry):
                xs = (x + t // 2) % 2
                h = t % 2
                if d == 0:
                    @pl.when(t >= 2)
                    def _():
                        self.arrived(z, xs, c, h)

                    @pl.when(has_up)
                    def _():
                        self.hop(0, z, xs, h, up).start()

                    @pl.when(has_down)
                    def _():
                        self.hop(1, z, xs, h, down).start()

                    self.hop(2, z, xs, h, sibling).start()
                else:
                    @pl.when(z - d >= 0)
                    def _():
                        zs = z - d
                        self.arrived(zs, xs, c, h)

                        @pl.when(has_up)
                        def _():
                            self.hop(0, zs, xs, h, up).start()

                        self.hop(2, zs, xs, h, sibling).start()

                    @pl.when(z + d < nz)
                    def _():
                        zs = z + d
                        self.arrived(zs, xs, c, h)

                        @pl.when(has_down)
                        def _():
                            self.hop(1, zs, xs, h, down).start()

                        self.hop(2, zs, xs, h, sibling).start()

                if work is not None:
                    work(t)
                return carry

            lax.fori_loop(first, last, one, 0)

        def sibling_part(self, zs):
            def one(t, carry):
                self.arrived(zs, (x + t // 2) % 2, oc, t % 2)
                return carry

            lax.fori_loop(0, 4, one, 0)

        def finish(self):
            for h in range(2):
                self.cross(h).wait_send()

            def one(t, carry):
                zs, xs, h = t // 4, (t // 2) % 2, t % 2

                @pl.when((zs <= z) & has_up)
                def _():
                    self.hop(0, zs, xs, h, up).wait_send()

                @pl.when((zs >= z) & has_down)
                def _():
                    self.hop(1, zs, xs, h, down).wait_send()

                self.hop(2, zs, xs, h, sibling).wait_send()
                return carry

            lax.fori_loop(0, nz * 4, one, 0)

    qkv = Ring(w_buf, wj_ref, w_send, w_recv, 0)
    outw = Ring(o_buf, wo_ref, o_send, o_recv, 2)

    for h in range(2):
        qkv.cross(h).start()
    for ring in (qkv, outw):
        for h in range(2):
            ring.own(h).start()
    for h in range(2):
        qkv.own(h).wait()
    qkv.forward(0, last=2)

    rows = hidden_ref[...].astype(jnp.float32)
    mean_square = jnp.mean(rows * rows, axis=-1, keepdims=True)
    mine = x * 2 + y
    act[mine] = (rows * lax.rsqrt(mean_square + norm_epsilon) * gain_ref[...]).astype(jnp.bfloat16)
    aux_buf[x] = aux_ref[...]

    def act_copy(k):
        px, py = flip(trio[k])
        return remote(act.at[mine], act.at[mine], act_send.at[k], act_recv.at[mine], dev(z, px, c, py))

    for k in range(3):
        act_copy(k).start()
    aux_copy = remote(aux_ref, aux_buf.at[x], x_send.at[4], x_recv.at[0], x_peer)
    aux_copy.start()
    qkv.forward(0, first=2)
    for h in range(2):
        outw.own(h).wait()

    rows_here = act.shape[0] * act.shape[1]
    span = act.shape[2] // nz
    width = acc.shape[1]
    acc[...] = jnp.zeros_like(acc)

    chunks = width // 256

    def project(zs, t):
        cols = pl.ds(pl.multiple_of(zs * span, span), span)

        def one(n, carry):
            at = pl.ds(pl.multiple_of(n * 256, 256), 256)
            left = act[:, :, cols].reshape(rows_here, span)
            right = w_buf[zs, :, :, :, :, at].reshape(span, 256)
            acc[:, at] += jnp.dot(left, right, preferred_element_type=jnp.float32)
            return carry

        @pl.when(t == 0)
        def _():
            qkv.sibling_part(zs)

        lax.fori_loop(t * chunks // 4, (t + 1) * chunks // 4, one, 0)

    def each(d, work):
        if d == 0:
            work(z)
        else:
            @pl.when(z - d >= 0)
            def _():
                work(z - d)

            @pl.when(z + d < nz)
            def _():
                work(z + d)

    def part_of(d, work):
        return lambda t: each(d, lambda zs: work(zs, t))

    def whole_of(d, work):
        def one(t, carry):
            part_of(d, work)(t)
            return carry

        lax.fori_loop(0, 4, one, 0)

    qkv.forward(1)
    for k in range(3):
        px, py = flip(trio[k])
        q = px * 2 + py
        remote(act.at[q], act.at[q], act_send.at[0], act_recv.at[q], sibling).wait_recv()
    for h in range(2):
        outw.cross(h).start()
    for d in range(2, nz):
        qkv.forward(d, part_of(d - 2, project))
    outw.forward(0)
    for d in range(nz - 2, nz):
        whole_of(d, project)

    aux_copy.wait_send()
    remote(aux_ref, aux_buf.at[ox], x_send.at[4], x_recv.at[0], x_peer).wait_recv()
    lane = lax.broadcasted_iota(jnp.int32, (256, HEAD), 1)
    row_at = lax.broadcasted_iota(jnp.int32, (256, 256), 0)
    key_at = lax.broadcasted_iota(jnp.int32, (256, 256), 1)
    query_width = att.shape[1]
    kv_heads = (width - query_width) // (2 * HEAD)
    group = query_width // HEAD // kv_heads

    def attend(t):
        p = (ox + t // kv_heads) % 2
        g = t % kv_heads
        table = aux_buf[p, 0:256, :]
        swapped = pltpu.roll(table, HEAD // 2, 1)
        cosine = jnp.where(lane < HEAD // 2, table, swapped)
        sine = jnp.where(lane < HEAD // 2, -swapped, table)
        seg = jnp.concatenate([aux_buf[p, 256:257, :], aux_buf[p, 257:258, :]], axis=1)
        seg_key = jnp.broadcast_to(seg, (256, 256))
        seg_row = seg_key.T
        allowed = ((seg_key == seg_row) & (seg_row >= 0) & (key_at <= row_at)) | (key_at == row_at)
        pack = pl.ds(pl.multiple_of(p * 256, 256), 256)

        def head_of(at):
            return acc[pack, pl.ds(pl.multiple_of(at * HEAD, HEAD), HEAD)]

        def turned(v):
            return (v * cosine + pltpu.roll(v, HEAD // 2, 1) * sine).astype(jnp.bfloat16)

        key = turned(head_of(query_width // HEAD + g))
        value = head_of(query_width // HEAD + kv_heads + g).astype(jnp.bfloat16)
        cache_send[p, :, pl.ds(pl.multiple_of(g * 256, 256), HEAD)] = key
        cache_send[p, :, pl.ds(pl.multiple_of(g * 256 + HEAD, HEAD), HEAD)] = value
        for i in range(group):
            query = turned(head_of(g * group + i))
            scores = lax.dot_general(
                query, key, (((1,), (1,)), ((), ())), preferred_element_type=jnp.float32
            ) * HEAD ** (-0.5)
            scores = jnp.where(allowed, scores, -1e30)
            weight = jnp.exp(scores - jnp.max(scores, axis=-1, keepdims=True))
            total = jnp.sum(weight, axis=-1, keepdims=True)
            mixed = jnp.dot(weight.astype(jnp.bfloat16), value, preferred_element_type=jnp.float32)
            att[pack, pl.ds(pl.multiple_of((g * group + i) * HEAD, HEAD), HEAD)] = (mixed / total).astype(
                jnp.bfloat16
            )

    outw.forward(1, attend)
    cache_copy = remote(cache_send.at[ox], cache_got, x_send.at[5], x_recv.at[1], x_peer)
    cache_copy.start()

    depth, cols_out = o_buf.shape[3] * o_buf.shape[4], o_buf.shape[5]

    def strip(n):
        return pl.ds(pl.multiple_of(n * cols_out, cols_out), cols_out)

    def sum_copy(zs, n, k):
        px, py = flip(trio[k])
        return remote(
            part.at[zs, px * 2 + py, :, strip(n)], got.at[zs, k, :, strip(n)],
            sum_send.at[zs, n, k], sum_recv.at[zs, n, k], dev(z, px, c, py),
        )

    def outward(zs, n):
        xs, cs = n // 2, n % 2

        @pl.when(cs == oc)
        def _():
            for h in range(2):
                outw.arrived(zs, xs, oc, h)

        right = o_buf[zs, xs, cs].reshape(depth, cols_out)
        product = jnp.dot(att[...], right, preferred_element_type=jnp.float32)
        part[zs, :, :, strip(n)] = product.astype(jnp.bfloat16).reshape(4, rows_here // 4, cols_out)
        for k in (2, 1, 0):
            sum_copy(zs, n, k).start()

    def final_strip(zs, k):
        outward(zs, (x + k // 2) % 2 * 2 + (c + k % 2) % 2)

    for d in range(2, nz):
        early = part_of(d - 2, outward)
        if d < nz - 1:
            outw.forward(d, early)
        else:
            late = part_of(d - 1, outward)

            def both(t):
                early(t)
                late(t)

                @pl.when(t > 0)
                def _():
                    each(d, lambda zs: final_strip(zs, t - 1))

            outw.forward(d, both)
    each(nz - 1, lambda zs: final_strip(zs, 3))

    cache_copy.wait()
    kept = cache_ref.shape[1] // 2
    cache_ref[:, pl.ds(pl.multiple_of(x * kept, kept), kept)] = cache_send[x]
    cache_ref[:, pl.ds(pl.multiple_of(ox * kept, kept), kept)] = cache_got[...]
    qkv.finish()
    outw.finish()
    for k in range(3):
        act_copy(k).wait_send()

    def settle(zs):
        for n in range(4):
            for k in range(3):
                sum_copy(zs, n, k).wait()
        cols = pl.ds(pl.multiple_of(zs * span, span), span)
        total = part[zs, mine].astype(jnp.float32)
        for k in range(3):
            total = total + got[zs, k].astype(jnp.float32)
        out_ref[:, cols] = (total + hidden_ref[:, cols].astype(jnp.float32)).astype(jnp.bfloat16)

    for d in range(nz):
        each(d, settle)


def fused_body(n_dp, hidden_in, norm_gain, w_query, w_key, w_value, w_out, segment):
    nz = n_dp // 4
    rows, features = hidden_in.shape
    pack_rows = segment.shape[0]
    depth, query_cols = w_query.shape
    kv_cols = w_key.shape[1]
    width = (query_cols + 2 * kv_cols) // 2
    out_cols = w_out.shape[1]

    def halves(w):
        return jnp.transpose(w.reshape(depth, 2, w.shape[1] // 2), (1, 0, 2))

    joined = jnp.concatenate((halves(w_query), halves(w_key), halves(w_value)), axis=2)
    joined = joined.reshape(2, 2, depth // 2, width)
    out_parts = w_out.reshape(2, 2, query_cols // 4, out_cols)
    angles = positions_of(segment).astype(jnp.float32)[:, None] * inverse_frequency(HEAD)[None, :]
    aux = jnp.concatenate(
        (
            jnp.cos(angles), jnp.sin(angles),
        ),
        axis=1,
    )
    aux = jnp.concatenate(
        (aux, segment.astype(jnp.float32).reshape(pack_rows // 128, 128), jnp.zeros((6, 128), jnp.float32)), axis=0
    )
    vmem = pl.BlockSpec(memory_space=pltpu.VMEM)
    dma = pltpu.SemaphoreType.DMA
    low = jnp.bfloat16
    hidden_out, cache = pl.pallas_call(
        functools.partial(fused_kernel, nz),
        out_shape=(
            jax.ShapeDtypeStruct((rows, features), low),
            jax.ShapeDtypeStruct((pack_rows, 2 * kv_cols), low),
        ),
        in_specs=[vmem] * 5,
        out_specs=(vmem, vmem),
        scratch_shapes=[
            pltpu.VMEM((4, rows, features), low),
            pltpu.VMEM((nz, 2, 2, 2, depth // 2, width), low),
            pltpu.VMEM((nz, 2, 2, 2, query_cols // 4, out_cols), low),
            pltpu.VMEM((2,) + aux.shape, jnp.float32),
            pltpu.VMEM((4 * rows, width), jnp.float32),
            pltpu.VMEM((4 * rows, query_cols // 2), low),
            pltpu.VMEM((nz, 4, rows, features // nz), low),
            pltpu.VMEM((nz, 3, rows, features // nz), low),
            pltpu.VMEM((2, pack_rows, kv_cols), low),
            pltpu.VMEM((pack_rows, kv_cols), low),
            dma((4,)), dma((6,)), dma((2,)), dma((3,)), dma((4,)),
            dma((3, nz, 2, 2)), dma((nz, 2, 2, 2)), dma((3, nz, 2, 2)), dma((nz, 2, 2, 2)),
            dma((nz, 4, 3)), dma((nz, 4, 3)),
        ],
        compiler_params=pltpu.CompilerParams(
            collective_id=0, has_side_effects=True, vmem_limit_bytes=60 * 1024 * 1024
        ),
    )(hidden_in, norm_gain.astype(jnp.float32).reshape(1, features), joined, out_parts, aux)
    return hidden_out, cache.reshape(pack_rows, kv_cols // HEAD, 2 * HEAD)


def solution(mesh):
    n_dp, n_tensor = mesh.shape["dp"], mesh.shape["tensor"]

    def chosen(*blocks):
        if n_tensor == 2 and n_dp % 4 == 0 and n_dp >= 12 and blocks[3].shape[1] == 4 * HEAD:
            return fused_body(n_dp, *blocks)
        return body(*blocks)

    return jax.shard_map(
        chosen,
        mesh=mesh,
        in_specs=(
            P(("dp", "tensor"), None),
            P(),
            P("dp", "tensor"),
            P("dp", "tensor"),
            P("dp", "tensor"),
            P("tensor", "dp"),
            P("dp"),
        ),
        out_specs=(P(("dp", "tensor"), None), P("dp", "tensor", None)),
        check_vma=False,
    )
```

```python
import functools

import jax
import jax.numpy as jnp
from jax import lax
from jax.experimental import pallas as pl
from jax.experimental.pallas import tpu as pltpu
from jax.sharding import PartitionSpec as P

HEAD = 128


rope_theta = 500000.0
norm_epsilon = 1e-05


def inverse_frequency(head_width):
    exponent = jnp.arange(0, head_width, 2).astype(jnp.float32) / head_width
    base_freq = rope_theta ** (-exponent)
    wavelength = 2.0 * jnp.pi / base_freq
    smooth = (8192.0 / wavelength - 1.0) / 3.0
    blended = (1.0 - smooth) * base_freq / 8.0 + smooth * base_freq
    return jnp.where(
        wavelength < 2048.0, base_freq, jnp.where(wavelength > 8192.0, base_freq / 8.0, blended)
    )


def positions_of(segment):
    row_index = jnp.arange(segment.shape[0], dtype=jnp.int32)
    changed = jnp.concatenate([jnp.ones((1,), dtype=bool), segment[1:] != segment[:-1]])
    earlier = changed[None, :] & (row_index[None, :] <= row_index[:, None])
    return row_index - jnp.max(jnp.where(earlier, row_index[None, :], 0), axis=1)


def rotate(vectors, position):
    head_width = vectors.shape[-1]
    half_width = head_width // 2
    angles = position.astype(jnp.float32)[:, None] * inverse_frequency(head_width)[None, :]
    cosine = jnp.concatenate([jnp.cos(angles), jnp.cos(angles)], axis=-1)[:, None, :]
    sine_table = jnp.concatenate([jnp.sin(angles), jnp.sin(angles)], axis=-1)[:, None, :]
    turned = jnp.concatenate([-vectors[..., half_width:], vectors[..., :half_width]], axis=-1)
    return vectors * cosine + turned * sine_table


def rms_normed(rows_float, norm_gain):
    mean_square = jnp.mean(rows_float * rows_float, axis=-1, keepdims=True)
    return (
        rows_float * lax.rsqrt(mean_square + norm_epsilon) * norm_gain.astype(jnp.float32)
    ).astype(jnp.bfloat16)


def visible_pairs(segment, key_count):
    row_index = jnp.arange(segment.shape[0], dtype=jnp.int32)
    key_index = jnp.arange(key_count, dtype=jnp.int32)
    same_segment = (segment[:, None] == segment[None, :]) & (segment[:, None] >= 0)
    causal = key_index[None, :] <= row_index[:, None]
    return same_segment & causal | (key_index[None, :] == row_index[:, None])


def body(hidden_in, norm_gain, w_query, w_key, w_value, w_out, segment):
    pack_rows = segment.shape[0]
    query_cols = w_query.shape[1]
    kv_cols = w_key.shape[1]
    query_heads = query_cols // HEAD
    kv_heads = kv_cols // HEAD
    group_size = query_heads // kv_heads
    score_scale = HEAD ** (-0.5)
    rows_float = hidden_in.astype(jnp.float32)
    normed = rms_normed(rows_float, norm_gain)
    gathered = lax.all_gather(normed, "tensor", axis=0, tiled=True)
    joined = jnp.concatenate(
        (
            lax.all_gather(w_query, "dp", axis=0, tiled=True),
            lax.all_gather(w_key, "dp", axis=0, tiled=True),
            lax.all_gather(w_value, "dp", axis=0, tiled=True),
        ),
        axis=1,
    )
    projected = jnp.dot(gathered, joined, preferred_element_type=jnp.float32)
    position = positions_of(segment)
    query_rows = rotate(
        projected[:, :query_cols].reshape(pack_rows, query_heads, HEAD), position
    ).astype(jnp.bfloat16)
    key_rows = rotate(
        projected[:, query_cols : query_cols + kv_cols].reshape(pack_rows, kv_heads, HEAD), position
    ).astype(jnp.bfloat16)
    value_rows = (
        projected[:, query_cols + kv_cols :].astype(jnp.bfloat16).reshape(pack_rows, kv_heads, HEAD)
    )
    cache_rows = jnp.concatenate([key_rows, value_rows], axis=-1)
    grouped_query = query_rows.reshape(pack_rows, kv_heads, group_size, HEAD)
    scores = (
        jnp.einsum("skgh,tkh->kgst", grouped_query, key_rows, preferred_element_type=jnp.float32)
        * score_scale
    )
    allowed = visible_pairs(segment, pack_rows)
    scores = jnp.where(allowed, scores, -1e30)
    row_max = jnp.max(scores, axis=-1, keepdims=True)
    weight = jnp.exp(scores - row_max)
    weight_sum = jnp.sum(weight, axis=-1)
    mixed_rows = (
        jnp.einsum(
            "kgst,tkh->kgsh",
            weight.astype(jnp.bfloat16),
            value_rows,
            preferred_element_type=jnp.float32,
        )
        / weight_sum[..., None]
    )
    attended = (
        jnp.transpose(mixed_rows, (2, 0, 1, 3)).astype(jnp.bfloat16).reshape(pack_rows, query_cols)
    )
    out_full = lax.all_gather(w_out, "dp", axis=1, tiled=True)
    summed = lax.psum_scatter(
        jnp.dot(attended, out_full, preferred_element_type=jnp.float32).astype(jnp.bfloat16),
        "tensor",
        scatter_dimension=0,
        tiled=True,
    ).astype(jnp.float32)
    hidden_out = (summed + rows_float).astype(jnp.bfloat16)
    return (hidden_out, cache_rows)


MESH = pl.DeviceIdType.MESH


def fused_kernel(
    nz, hidden_ref, gain_ref, wq_ref, wk_ref, wv_ref, wo_ref, aux_ref,
    out_ref, cache_ref,
    act, w_buf, o_buf, aux_buf, acc, att, part, got, cache_send, cache_got,
    local_sem, x_send, x_recv, act_send, act_recv,
    w_send, w_recv, o_send, o_recv, sum_send, sum_recv,
):
    dp = lax.axis_index("dp")
    y = lax.axis_index("tensor")
    z = dp // 4
    x = (dp // 2) % 2
    c = dp % 2
    ox, oy, oc = 1 - x, 1 - y, 1 - c

    def dev(zz, xx, cc, yy):
        return {"dp": zz * 4 + xx * 2 + cc, "tensor": yy}

    x_peer = dev(z, ox, c, y)
    sibling = dev(z, x, oc, y)
    has_up = z + 1 < nz
    has_down = z > 0
    up = dev(jnp.minimum(z + 1, nz - 1), x, c, y)
    down = dev(jnp.maximum(z - 1, 0), x, c, y)
    trio = ((0, 1), (1, 0), (1, 1))

    def flip(delta):
        return (x + delta[0]) % 2, (y + delta[1]) % 2

    barrier = pltpu.get_barrier_semaphore()
    for delta in trio:
        px, py = flip(delta)
        pl.semaphore_signal(barrier, inc=1, device_id=dev(z, px, c, py), device_id_type=MESH)
    pl.semaphore_signal(barrier, inc=1, device_id=sibling, device_id_type=MESH)

    @pl.when(has_up)
    def _():
        pl.semaphore_signal(barrier, inc=1, device_id=up, device_id_type=MESH)

    @pl.when(has_down)
    def _():
        pl.semaphore_signal(barrier, inc=1, device_id=down, device_id_type=MESH)

    pl.semaphore_wait(barrier, 4 + jnp.where(has_up, 1, 0) + jnp.where(has_down, 1, 0))

    def remote(src, dst, send, recv, device):
        return pltpu.make_async_remote_copy(
            src_ref=src, dst_ref=dst, send_sem=send, recv_sem=recv, device_id=device, device_id_type=MESH
        )

    class Ring:
        def __init__(self, buf, src, send, recv, at):
            self.buf, self.src, self.send, self.recv, self.at = buf, src, send, recv, at

        def pieces(self, xx, h):
            slot = self.buf.at[z, x, c, h]
            if len(self.src) == 1:
                return [(self.src[0].at[xx, h], slot)]
            found, start = [], 0
            for ref in self.src:
                tall, wide = ref.shape[0] // 2, ref.shape[1] // 2
                cols = pl.ds(pl.multiple_of(xx * wide, wide), wide)
                found.append(
                    (ref.at[pl.ds(h * tall, tall), cols], self.buf.at[z, x, c, h, :, pl.ds(start, wide)])
                )
                start += wide
            return found

        def own(self, h):
            found = self.pieces(x, h)
            at = self.at + h * len(found)
            return [pltpu.make_async_copy(a, b, local_sem.at[at + i]) for i, (a, b) in enumerate(found)]

        def cross(self, h):
            found = self.pieces(ox, h)
            at = self.at + h * len(found)
            return [
                remote(a, b, x_send.at[at + i], self.recv.at[z, x, c, h], x_peer)
                for i, (a, b) in enumerate(found)
            ]

        def hop(self, way, zs, xs, h, device):
            slot = self.buf.at[zs, xs, c, h]
            return remote(slot, slot, self.send.at[way, zs, xs, h], self.recv.at[zs, xs, c, h], device)

        def arrived(self, zs, xs, cc, h):
            slot = self.buf.at[zs, xs, cc, h]
            remote(slot, slot, self.send.at[0, 0, 0, 0], self.recv.at[zs, xs, cc, h], sibling).wait_recv()

        def forward(self, d, work=None, first=0, last=4):
            def one(t, carry):
                xs = (x + t // 2) % 2
                h = t % 2
                if d == 0:
                    @pl.when(t >= 2)
                    def _():
                        self.arrived(z, xs, c, h)

                    @pl.when(has_up)
                    def _():
                        self.hop(0, z, xs, h, up).start()

                    @pl.when(has_down)
                    def _():
                        self.hop(1, z, xs, h, down).start()

                    self.hop(2, z, xs, h, sibling).start()
                else:
                    @pl.when(z - d >= 0)
                    def _():
                        zs = z - d
                        self.arrived(zs, xs, c, h)

                        @pl.when(has_up)
                        def _():
                            self.hop(0, zs, xs, h, up).start()

                        self.hop(2, zs, xs, h, sibling).start()

                    @pl.when(z + d < nz)
                    def _():
                        zs = z + d
                        self.arrived(zs, xs, c, h)

                        @pl.when(has_down)
                        def _():
                            self.hop(1, zs, xs, h, down).start()

                        self.hop(2, zs, xs, h, sibling).start()

                if work is not None:
                    work(t)
                return carry

            lax.fori_loop(first, last, one, 0)

        def sibling_part(self, zs):
            def one(t, carry):
                self.arrived(zs, (x + t // 2) % 2, oc, t % 2)
                return carry

            lax.fori_loop(0, 4, one, 0)

        def finish(self):
            for h in range(2):
                for copy in self.cross(h):
                    copy.wait_send()

            def one(t, carry):
                zs, xs, h = t // 4, (t // 2) % 2, t % 2

                @pl.when((zs <= z) & has_up)
                def _():
                    self.hop(0, zs, xs, h, up).wait_send()

                @pl.when((zs >= z) & has_down)
                def _():
                    self.hop(1, zs, xs, h, down).wait_send()

                self.hop(2, zs, xs, h, sibling).wait_send()
                return carry

            lax.fori_loop(0, nz * 4, one, 0)

    qkv = Ring(w_buf, (wq_ref, wk_ref, wv_ref), w_send, w_recv, 0)
    outw = Ring(o_buf, (wo_ref,), o_send, o_recv, 6)

    for h in range(2):
        for copy in qkv.cross(h):
            copy.start()
    for ring in (qkv, outw):
        for h in range(2):
            for copy in ring.own(h):
                copy.start()
    for h in range(2):
        for copy in qkv.own(h):
            copy.wait()
    qkv.forward(0, last=2)

    rows = hidden_ref[...].astype(jnp.float32)
    mean_square = jnp.mean(rows * rows, axis=-1, keepdims=True)
    mine = x * 2 + y
    act[mine] = (rows * lax.rsqrt(mean_square + norm_epsilon) * gain_ref[...]).astype(jnp.bfloat16)
    aux_buf[x] = aux_ref[...]

    def act_copy(k):
        px, py = flip(trio[k])
        return remote(act.at[mine], act.at[mine], act_send.at[k], act_recv.at[mine], dev(z, px, c, py))

    for k in range(3):
        act_copy(k).start()
    aux_copy = remote(aux_ref, aux_buf.at[x], x_send.at[8], x_recv.at[0], x_peer)
    aux_copy.start()
    qkv.forward(0, first=2)
    for h in range(2):
        for copy in outw.own(h):
            copy.wait()

    rows_here = act.shape[0] * act.shape[1]
    span = act.shape[2] // nz
    width = acc.shape[1]
    acc[...] = jnp.zeros_like(acc)

    chunks = width // 256

    def project(zs, t):
        cols = pl.ds(pl.multiple_of(zs * span, span), span)

        def one(n, carry):
            at = pl.ds(pl.multiple_of(n * 256, 256), 256)
            left = act[:, :, cols].reshape(rows_here, span)
            right = w_buf[zs, :, :, :, :, at].reshape(span, 256)
            acc[:, at] += jnp.dot(left, right, preferred_element_type=jnp.float32)
            return carry

        @pl.when(t == 0)
        def _():
            qkv.sibling_part(zs)

        lax.fori_loop(t * chunks // 4, (t + 1) * chunks // 4, one, 0)

    def each(d, work):
        if d == 0:
            work(z)
        else:
            @pl.when(z - d >= 0)
            def _():
                work(z - d)

            @pl.when(z + d < nz)
            def _():
                work(z + d)

    def part_of(d, work):
        return lambda t: each(d, lambda zs: work(zs, t))

    def whole_of(d, work):
        def one(t, carry):
            part_of(d, work)(t)
            return carry

        lax.fori_loop(0, 4, one, 0)

    qkv.forward(1)
    for k in range(3):
        px, py = flip(trio[k])
        q = px * 2 + py
        remote(act.at[q], act.at[q], act_send.at[0], act_recv.at[q], sibling).wait_recv()
    for h in range(2):
        for copy in outw.cross(h):
            copy.start()
    for d in range(2, nz):
        qkv.forward(d, part_of(d - 2, project))
    outw.forward(0)
    for d in range(nz - 2, nz):
        whole_of(d, project)

    aux_copy.wait_send()
    remote(aux_ref, aux_buf.at[ox], x_send.at[8], x_recv.at[0], x_peer).wait_recv()
    lane = lax.broadcasted_iota(jnp.int32, (256, HEAD), 1)
    row_at = lax.broadcasted_iota(jnp.int32, (256, 256), 0)
    key_at = lax.broadcasted_iota(jnp.int32, (256, 256), 1)
    query_width = att.shape[1]
    kv_heads = (width - query_width) // (2 * HEAD)
    group = query_width // HEAD // kv_heads

    def attend(t):
        p = (ox + t // kv_heads) % 2
        g = t % kv_heads
        table = aux_buf[p, 0:256, :]
        swapped = pltpu.roll(table, HEAD // 2, 1)
        cosine = jnp.where(lane < HEAD // 2, table, swapped)
        sine = jnp.where(lane < HEAD // 2, -swapped, table)
        seg = jnp.concatenate([aux_buf[p, 256:257, :], aux_buf[p, 257:258, :]], axis=1)
        seg_key = jnp.broadcast_to(seg, (256, 256))
        seg_row = seg_key.T
        allowed = ((seg_key == seg_row) & (seg_row >= 0) & (key_at <= row_at)) | (key_at == row_at)
        pack = pl.ds(pl.multiple_of(p * 256, 256), 256)

        def head_of(at):
            return acc[pack, pl.ds(pl.multiple_of(at * HEAD, HEAD), HEAD)]

        def turned(v):
            return (v * cosine + pltpu.roll(v, HEAD // 2, 1) * sine).astype(jnp.bfloat16)

        key = turned(head_of(query_width // HEAD + g))
        value = head_of(query_width // HEAD + kv_heads + g).astype(jnp.bfloat16)
        cache_send[p, :, pl.ds(pl.multiple_of(g * 256, 256), HEAD)] = key
        cache_send[p, :, pl.ds(pl.multiple_of(g * 256 + HEAD, HEAD), HEAD)] = value
        for i in range(group):
            query = turned(head_of(g * group + i))
            scores = lax.dot_general(
                query, key, (((1,), (1,)), ((), ())), preferred_element_type=jnp.float32
            ) * HEAD ** (-0.5)
            scores = jnp.where(allowed, scores, -1e30)
            weight = jnp.exp(scores - jnp.max(scores, axis=-1, keepdims=True))
            total = jnp.sum(weight, axis=-1, keepdims=True)
            mixed = jnp.dot(weight.astype(jnp.bfloat16), value, preferred_element_type=jnp.float32)
            att[pack, pl.ds(pl.multiple_of((g * group + i) * HEAD, HEAD), HEAD)] = (mixed / total).astype(
                jnp.bfloat16
            )

    outw.forward(1, attend)
    cache_copy = remote(cache_send.at[ox], cache_got, x_send.at[9], x_recv.at[1], x_peer)
    cache_copy.start()

    depth, cols_out = o_buf.shape[3] * o_buf.shape[4], o_buf.shape[5]

    def strip(n):
        return pl.ds(pl.multiple_of(n * cols_out, cols_out), cols_out)

    def sum_copy(zs, n, k):
        px, py = flip(trio[k])
        return remote(
            part.at[zs, px * 2 + py, :, strip(n)], got.at[zs, k, :, strip(n)],
            sum_send.at[zs, n, k], sum_recv.at[zs, n, k], dev(z, px, c, py),
        )

    def outward(zs, n):
        xs, cs = n // 2, n % 2

        @pl.when(cs == oc)
        def _():
            for h in range(2):
                outw.arrived(zs, xs, oc, h)

        right = o_buf[zs, xs, cs].reshape(depth, cols_out)
        product = jnp.dot(att[...], right, preferred_element_type=jnp.float32)
        part[zs, :, :, strip(n)] = product.astype(jnp.bfloat16).reshape(4, rows_here // 4, cols_out)
        for k in (2, 1, 0):
            sum_copy(zs, n, k).start()

    def final_strip(zs, k):
        outward(zs, (x + k // 2) % 2 * 2 + (c + k % 2) % 2)

    for d in range(2, nz):
        early = part_of(d - 2, outward)
        if d < nz - 1:
            outw.forward(d, early)
        else:
            late = part_of(d - 1, outward)

            def both(t):
                early(t)
                late(t)

                @pl.when(t > 0)
                def _():
                    each(d, lambda zs: final_strip(zs, t - 1))

            outw.forward(d, both)
    each(nz - 1, lambda zs: final_strip(zs, 3))

    cache_copy.wait()
    kept = cache_ref.shape[1] // 2
    cache_ref[:, pl.ds(pl.multiple_of(x * kept, kept), kept)] = cache_send[x]
    cache_ref[:, pl.ds(pl.multiple_of(ox * kept, kept), kept)] = cache_got[...]
    qkv.finish()
    outw.finish()
    for k in range(3):
        act_copy(k).wait_send()

    def settle(zs):
        for n in range(4):
            for k in range(3):
                sum_copy(zs, n, k).wait()
        cols = pl.ds(pl.multiple_of(zs * span, span), span)
        total = part[zs, mine].astype(jnp.float32)
        for k in range(3):
            total = total + got[zs, k].astype(jnp.float32)
        out_ref[:, cols] = (total + hidden_ref[:, cols].astype(jnp.float32)).astype(jnp.bfloat16)

    for d in range(nz):
        each(d, settle)


def fused_body(n_dp, hidden_in, norm_gain, w_query, w_key, w_value, w_out, segment):
    nz = n_dp // 4
    rows, features = hidden_in.shape
    pack_rows = segment.shape[0]
    depth, query_cols = w_query.shape
    kv_cols = w_key.shape[1]
    width = (query_cols + 2 * kv_cols) // 2
    out_cols = w_out.shape[1]

    out_parts = w_out.reshape(2, 2, query_cols // 4, out_cols)
    angles = positions_of(segment).astype(jnp.float32)[:, None] * inverse_frequency(HEAD)[None, :]
    aux = jnp.concatenate(
        (
            jnp.cos(angles), jnp.sin(angles),
        ),
        axis=1,
    )
    aux = jnp.concatenate(
        (aux, segment.astype(jnp.float32).reshape(pack_rows // 128, 128), jnp.zeros((6, 128), jnp.float32)), axis=0
    )
    vmem = pl.BlockSpec(memory_space=pltpu.VMEM)
    dma = pltpu.SemaphoreType.DMA
    low = jnp.bfloat16
    hidden_out, cache = pl.pallas_call(
        functools.partial(fused_kernel, nz),
        out_shape=(
            jax.ShapeDtypeStruct((rows, features), low),
            jax.ShapeDtypeStruct((pack_rows, 2 * kv_cols), low),
        ),
        in_specs=[vmem] * 7,
        out_specs=(vmem, vmem),
        scratch_shapes=[
            pltpu.VMEM((4, rows, features), low),
            pltpu.VMEM((nz, 2, 2, 2, depth // 2, width), low),
            pltpu.VMEM((nz, 2, 2, 2, query_cols // 4, out_cols), low),
            pltpu.VMEM((2,) + aux.shape, jnp.float32),
            pltpu.VMEM((4 * rows, width), jnp.float32),
            pltpu.VMEM((4 * rows, query_cols // 2), low),
            pltpu.VMEM((nz, 4, rows, features // nz), low),
            pltpu.VMEM((nz, 3, rows, features // nz), low),
            pltpu.VMEM((2, pack_rows, kv_cols), low),
            pltpu.VMEM((pack_rows, kv_cols), low),
            dma((8,)), dma((10,)), dma((2,)), dma((3,)), dma((4,)),
            dma((3, nz, 2, 2)), dma((nz, 2, 2, 2)), dma((3, nz, 2, 2)), dma((nz, 2, 2, 2)),
            dma((nz, 4, 3)), dma((nz, 4, 3)),
        ],
        compiler_params=pltpu.CompilerParams(
            collective_id=0, has_side_effects=True, vmem_limit_bytes=60 * 1024 * 1024
        ),
    )(hidden_in, norm_gain.astype(jnp.float32).reshape(1, features), w_query, w_key, w_value, out_parts, aux)
    return hidden_out, cache.reshape(pack_rows, kv_cols // HEAD, 2 * HEAD)


def solution(mesh):
    n_dp, n_tensor = mesh.shape["dp"], mesh.shape["tensor"]

    def chosen(*blocks):
        if n_tensor == 2 and n_dp % 4 == 0 and n_dp >= 12 and blocks[3].shape[1] == 4 * HEAD:
            return fused_body(n_dp, *blocks)
        return body(*blocks)

    return jax.shard_map(
        chosen,
        mesh=mesh,
        in_specs=(
            P(("dp", "tensor"), None),
            P(),
            P("dp", "tensor"),
            P("dp", "tensor"),
            P("dp", "tensor"),
            P("tensor", "dp"),
            P("dp"),
        ),
        out_specs=(P(("dp", "tensor"), None), P("dp", "tensor", None)),
        check_vma=False,
    )
```
